512 devices in a mesh: group: 16 (over z_lo, x), fsdp: 32 (over y, z_hi, core).
Axes of the slice: x: 4, y: 4, z: 16 (z_hi: 4, z_lo: 4; z = z_hi * 4 + z_lo), core: 2. Of those that a mesh axis runs over, the one named last changes fastest.
Arguments:
- hidden: bfloat16 [24576, 4608], P(('group', 'fsdp')), may hold values from -20 to 20
- down_w: bfloat16 [16, 2304, 4608], P('group', 'fsdp'), may hold values from -20 to 20
- moment_one: bfloat16 [16, 2304, 4608], P('group', 'fsdp'), may hold values from -0.75 to 0.75
- moment_two: bfloat16 [16, 2304, 4608], P('group', 'fsdp'), may hold values from 0.0049743652 to 0.049804688
- norm_gain: bfloat16 [2304], replicated, may hold values from 0.099609375 to 1.8984375
- cotangent: bfloat16 [24576, 2304], P(('group', 'fsdp')), may hold values from -6 to 6
- frag_delta: bfloat16 [16, 2304, 1024], P('group', 'fsdp'), may hold values from -6 to 6
- outer_params: float32 [2304, 1024], P('fsdp'), may hold values from -6 to 6
- outer_momentum: float32 [2304, 1024], P('fsdp'), may hold values from -6 to 6
Outputs:
- normed: bfloat16 [24576, 2304], P(('group', 'fsdp'))
- adam_step: bfloat16 [16, 2304, 4608], P('group', 'fsdp')
- new_outer: float32 [2304, 1024], P('fsdp')
The draws below stay inside these ranges and needn't reach their ends.
All inputs are finite; a program needn't handle non-finite values.
Results may differ from the reference program's by a relative error of at most 0.0065.
Values may be sent and summed in bfloat16 or wider, within the bound.
A program may use at most 64 MiB of HBM per device.

```python
import math
import jax
import jax.numpy as jnp
from jax import lax

D = 2304
KV = 1024
HID = 4608
GROUP_TOK = 1536
TOKENS = 24576
N_GROUP = 16


def draw_hidden(key, part):
    key = jax.random.fold_in(key, 11)
    first, second = jax.random.split(key, 2)
    base = jnp.clip(jax.random.normal(first, (TOKENS, HID), jnp.float32), -6.0, 6.0)
    scale = 10.0 ** jax.random.uniform(second, (TOKENS, 1), jnp.float32, -0.5, 0.5)
    return (base * scale).astype(jnp.bfloat16)


def draw_down_w(key, part):
    key = jax.random.fold_in(key, 23)
    first = jax.random.fold_in(key, 0)
    position = jnp.arange(D, dtype=jnp.float32) / D
    base = jnp.clip(jax.random.normal(first, (N_GROUP, D, HID), jnp.float32), -6.0, 6.0)
    rise = 10.0 ** (position - 0.5)
    return (base * rise[None, :, None]).astype(jnp.bfloat16)


def block_levels(stream_key, dims, cuts, low, top_value):
    def one(dim, shards_of):
        steps = jax.random.uniform(jax.random.fold_in(jax.random.fold_in(stream_key, 6), dim), (shards_of,), jnp.float32, low / len(cuts), top_value / len(cuts))
        return jnp.repeat(jnp.exp(steps), dims[dim] // shards_of).reshape((-1,) + (1,) * (len(dims) - dim - 1))

    factor_of = one(*cuts[0])
    for cut in cuts[1:]:
        factor_of = factor_of * one(*cut)
    return factor_of


def gaussian(rng, shape, deviation, most, pieces=(), kind=jnp.bfloat16):
    values = deviation * jax.random.normal(rng, shape, jnp.float32)
    if pieces:
        values = values * block_levels(rng, shape, pieces, -0.22, 0.18)
    return jnp.clip(values, -most, most).astype(kind)


def setup_inputs(seed: int = 0) -> dict:
    seeds = jax.random.split(jax.random.key(seed), 10)
    return {
        "hidden": draw_hidden(jax.random.fold_in(seeds[9], 71), 0),
        "down_w": draw_down_w(jax.random.fold_in(seeds[9], 71), 0),
        "moment_one": gaussian(seeds[2], (N_GROUP, D, HID), 0.05, 0.75, ((0, 16), (1, 32))),
        "moment_two": jnp.clip(jnp.exp(math.log(0.049804688) - 2.3038113 * jax.random.uniform(seeds[3], (N_GROUP, D, HID), jnp.float32) ** block_levels(seeds[3], (N_GROUP, D, HID), ((0, 16), (1, 32)), -0.2, 0.2)), 0.0049743652, 0.049804688).astype(jnp.bfloat16),
        "norm_gain": jnp.clip(1.0 + 0.18 * jax.random.normal(seeds[4], (D,), jnp.float32), 0.099609375, 1.8984375).astype(jnp.bfloat16),
        "cotangent": gaussian(seeds[5], (TOKENS, D), 1.0, 6.0, ((0, 512),)),
        "frag_delta": gaussian(seeds[6], (N_GROUP, D, KV), 1.0, 6.0, ((0, 16), (1, 32))),
        "outer_params": gaussian(seeds[7], (D, KV), 1.0, 6.0, ((0, 32),), jnp.float32),
        "outer_momentum": gaussian(seeds[8], (D, KV), 0.5, 6.0, ((0, 32),), jnp.float32),
    }


def reference(hidden, down_w, moment_one, moment_two, norm_gain, cotangent, frag_delta, outer_params, outer_momentum):
    gain = norm_gain.astype(jnp.float32)

    def one_group(items):
        rows, weight, first, second, cot = items
        y_val = jnp.dot(rows, weight.T, preferred_element_type=jnp.float32).astype(jnp.bfloat16)
        y_f = y_val.astype(jnp.float32)
        scale = lax.rsqrt(lax.optimization_barrier(jnp.mean(y_f * y_f, axis=1, keepdims=True)) + 1e-06)
        normed = (y_f * scale * gain).astype(jnp.bfloat16)
        weighted = gain * cot.astype(jnp.float32)
        cross = lax.optimization_barrier(jnp.mean(y_f * weighted, axis=1, keepdims=True))
        d_out = (scale * (weighted - y_f * scale * scale * cross)).astype(jnp.bfloat16)
        grad = jnp.dot(d_out.T, rows, preferred_element_type=jnp.float32)
        first_new = 0.9 * first.astype(jnp.float32) + 0.1 * grad
        second_new = 0.95 * second.astype(jnp.float32) + 0.05 * grad * grad
        step = first_new / (jnp.sqrt(second_new) + 1e-08) + 0.1 * weight.astype(jnp.float32)
        return (normed, step.astype(jnp.bfloat16))
    rows_all = hidden.reshape(N_GROUP, GROUP_TOK, HID)
    cot_all = cotangent.reshape(N_GROUP, GROUP_TOK, D)
    normed, adam_step = lax.map(one_group, (rows_all, down_w, moment_one, moment_two, cot_all))
    normed = normed.reshape(TOKENS, D)
    average = lax.optimization_barrier(jnp.sum(frag_delta.astype(jnp.float32), axis=0)) / N_GROUP
    momentum = 0.9 * outer_momentum + average
    new_outer = outer_params - 0.7 * (average + 0.9 * momentum)
    return (normed, adam_step, new_outer)
```

```python
import jax
import jax.numpy as jnp
from jax import lax
from jax.experimental import pallas as pl
from jax.experimental.pallas import tpu as pltpu
from jax.sharding import PartitionSpec as P

MESH = pl.DeviceIdType.MESH
F32 = jnp.float32
BF16 = jnp.bfloat16
D = 2304
HID = 4608
HALF = HID // 2
ROWS = 72
FEAT = 2 * ROWS
PAD = 80
PH = 3
TK = 256
CH = 1152
NCH = HID // CH


def body(
    h_in, w_in, m1_in, m2_in, gain_in, cot_in, delta_in, op_in, om_in,
    norm_out, adam_out, outer_out,
    hs, wp, w_own, m1, m2, grad, grad_in,
    cot_send, cot_recv, gain_rows, st_send, st_recv, a_keep, y_keep, ext_keep,
    ym_send, ym_recv, ye_send, ye_recv,
    d_own, d_recv, z_send, z_recv, o_own, o_recv, op, om,
    loc, zs_s, zs_r, zx_s, zx_r, ys_s, ys_r, yx_s, yx_r,
    w_s, w_r, cot_s, cot_r, st_s, st_r, ym_s, ym_r, ye_s, ye_r, g_s, g_r,
    dx_s, dx_r, dz_s, dz_r, do_s, do_r,
):
    g = lax.axis_index("group")
    f = lax.axis_index("fsdp")
    x, zl = lax.rem(g, 4), g // 4
    y, w, c = f // 8, lax.rem(f // 2, 4), lax.rem(f, 2)

    def dev(yy, ww, cc=None):
        return (g, yy * 8 + ww * 2 + (c if cc is None else cc))

    def far(xx, zz):
        return (zz * 4 + xx, f)

    def mod4(v):
        return lax.rem(v + 4, 4)

    def peer(o):
        return mod4(y + o // 4), mod4(w + lax.rem(o, 4))

    def rows16(s):
        return pl.ds(pl.multiple_of(s * 16, 16), 16)

    me = w * 4 + y
    mj = y * 4 + w
    yp, ym, wn, wm, wo = mod4(y + 1), mod4(y - 1), mod4(w + 1), mod4(w - 1), mod4(w + 2)
    yo = mod4(y + 2)

    sent = []

    def send(src, dst, s_sem, r_sem, where):
        cp = pltpu.make_async_remote_copy(
            src_ref=src, dst_ref=dst, send_sem=s_sem, recv_sem=r_sem,
            device_id=where, device_id_type=MESH,
        )
        cp.start()
        sent.append(cp)

    def arrived(dst, s_sem, r_sem, where):
        pltpu.make_async_remote_copy(
            src_ref=dst, dst_ref=dst, send_sem=s_sem, recv_sem=r_sem,
            device_id=where, device_id_type=MESH,
        ).wait_recv()

    barrier = pltpu.get_barrier_semaphore()

    @pl.loop(1, 16)
    def _(o):
        pl.semaphore_signal(barrier, inc=1, device_id=dev(*peer(o)), device_id_type=MESH)

    pl.semaphore_signal(barrier, inc=1, device_id=dev(y, w, 1 - c), device_id_type=MESH)
    for k in range(1, 4):
        pl.semaphore_signal(barrier, inc=1, device_id=far(mod4(x + k), zl), device_id_type=MESH)
        pl.semaphore_signal(barrier, inc=1, device_id=far(x, mod4(zl + k)), device_id_type=MESH)

    local = [
        pltpu.make_async_copy(h_in.at[pl.ds(16 * p, 16)], hs.at[p, rows16(me)], loc.at[p])
        for p in range(PH)
    ]
    local += [
        pltpu.make_async_copy(w_in, w_own, loc.at[3]),
        pltpu.make_async_copy(m1_in, m1, loc.at[4]),
        pltpu.make_async_copy(m2_in, m2, loc.at[5]),
        pltpu.make_async_copy(op_in, op, loc.at[6]),
        pltpu.make_async_copy(om_in, om, loc.at[7]),
    ]
    for cp in local:
        cp.start()

    zero = jnp.zeros((16, 80), F32)
    for j in range(16):
        part = cot_in[:, FEAT * j : FEAT * (j + 1)].astype(F32)
        tail = part[:, 128:]
        tail = jnp.concatenate([tail[0:16], tail[16:32], tail[32:48], zero], axis=1)
        cot_send[j] = jnp.concatenate([part[:, :128], tail], axis=0).astype(BF16)
        gj = gain_in[:, FEAT * j : FEAT * (j + 1)].astype(F32)
        gain_rows[j, 0:1, :] = gj[:, :128]
        gain_rows[j, 1:2, :] = jnp.concatenate([gj[:, 128:], jnp.zeros((1, 112), F32)], axis=1)
    delta = delta_in[...].astype(F32)
    for k in range(4):
        d_own[k] = delta[:, 256 * k : 256 * (k + 1)]
    local[3].wait()
    w32 = w_own[...].astype(F32)
    wp[c] = jnp.concatenate([w32, jnp.zeros((PAD - ROWS, HID), F32)], axis=0).astype(BF16)

    pl.semaphore_wait(barrier, 22)

    def own(p):
        src = h_in.at[pl.ds(16 * p, 16)]
        dst = hs.at[p, rows16(me)]
        send(src, dst, zs_s.at[p, 0], zs_r.at[p, 0], dev(y, wn))
        send(src, dst, zs_s.at[p, 1], zs_r.at[p, 1], dev(y, wm))
        spread(p, 0, src)

    def spread(p, q, src=None):
        slot = (w, wm, wn, wo)[q] * 4 + y
        dst = hs.at[p, rows16(slot)]
        src = dst if src is None else src
        send(src, dst, ys_s.at[p, q, 0], ys_r.at[p, q, 0], dev(yp, w))
        send(src, dst, ys_s.at[p, q, 1], ys_r.at[p, q, 1], dev(ym, w))

    def half(k):
        return pl.ds(k * HALF, HALF)

    def relay_z(p):
        for k, (came, to) in enumerate(((wm, wn), (wn, wm))):
            blk = hs.at[p, rows16(came * 4 + y)]
            arrived(blk, zs_s.at[p, k], zs_r.at[p, k], dev(y, to))
            part = hs.at[p, rows16(came * 4 + y), half(k)]
            send(part, part, zx_s.at[p, k], zx_r.at[p, k], dev(y, to))

    def got_z(p):
        for k, to in enumerate((wn, wm)):
            part = hs.at[p, rows16(wo * 4 + y), half(k)]
            arrived(part, zx_s.at[p, k], zx_r.at[p, k], dev(y, to))

    def relay_y(p, q):
        ww = (w, wm, wn, wo)[q]
        for k, (came, to) in enumerate(((ym, yp), (yp, ym))):
            blk = hs.at[p, rows16(ww * 4 + came)]
            arrived(blk, ys_s.at[p, q, k], ys_r.at[p, q, k], dev(to, w))
            part = hs.at[p, rows16(ww * 4 + came), half(k)]
            send(part, part, yx_s.at[p, q, k], yx_r.at[p, q, k], dev(to, w))

    def got_y(p):
        for q, ww in enumerate((w, wm, wn, wo)):
            for k, to in enumerate((yp, ym)):
                part = hs.at[p, rows16(ww * 4 + yo), half(k)]
                arrived(part, yx_s.at[p, q, k], yx_r.at[p, q, k], dev(to, w))

    own(0)
    send(wp.at[c], wp.at[c], w_s.at[0], w_r.at[0], dev(y, w, 1 - c))

    def cot_copy(o):
        yy, ww = peer(o)
        return pltpu.make_async_remote_copy(
            src_ref=cot_send.at[yy * 4 + ww], dst_ref=cot_recv.at[me],
            send_sem=cot_s.at[o], recv_sem=cot_r.at[me],
            device_id=dev(yy, ww), device_id_type=MESH,
        )

    @pl.loop(1, 16)
    def _(o):
        cot_copy(o).start()

    for k in range(1, 4):
        xx = mod4(x + k)
        send(d_own.at[xx], d_recv.at[x], dx_s.at[k], dx_r.at[x], far(xx, zl))
    own(1)
    cot_recv[me] = cot_send[mj]
    d_recv[x] = d_own[x]

    relay_z(0)
    spread(0, 1)
    spread(0, 2)
    relay_y(0, 0)
    own(2)
    relay_y(0, 1)
    relay_y(0, 2)

    for k in range(1, 4):
        xx = mod4(x + k)
        arrived(d_recv.at[xx], dx_s.at[k], dx_r.at[xx], far(xx, zl))
    part_x = d_recv[0] + d_recv[1] + d_recv[2] + d_recv[3]
    z_send[...] = jnp.concatenate([part_x, jnp.zeros((PAD - ROWS, 256), F32)], axis=0).astype(BF16)
    z_recv[zl] = z_send[...]
    for k in range(1, 4):
        zz = mod4(zl + k)
        send(z_send, z_recv.at[zl], dz_s.at[k], dz_r.at[zl], far(x, zz))

    got_z(0)
    spread(0, 3)

    arrived(wp.at[1 - c], w_s.at[0], w_r.at[0], dev(y, w, 1 - c))

    @pl.loop(1, 16)
    def _(o):
        yy, ww = peer(o)
        arrived(cot_recv.at[ww * 4 + yy], cot_s.at[o], cot_r.at[ww * 4 + yy], dev(yy, ww))

    gt = gain_rows[mj]
    gmain = jnp.broadcast_to(gt[0:1, :], (128, 128)).T
    gext = jnp.broadcast_to(gt[1:2, :], (128, 128)).T
    gcol = jnp.concatenate([gmain, gext[0:16]], axis=0)
    gcol = jnp.concatenate([gcol, gcol], axis=1)
    ext_all = cot_recv[:, 48:64, :].reshape(TK, 128).astype(F32).T
    for p in range(PH):
        main = cot_recv[:, 16 * p : 16 * p + 16, :].reshape(TK, 128).astype(F32).T
        a_keep[p] = gcol * jnp.concatenate([main, ext_all[16 * p : 16 * p + 16]], axis=0)
    local[0].wait()
    local[1].wait()
    local[2].wait()

    def st_copy(p, o):
        yy, ww = peer(o)
        return pltpu.make_async_remote_copy(
            src_ref=st_send.at[p], dst_ref=st_recv.at[p, mj],
            send_sem=st_s.at[p, o], recv_sem=st_r.at[p, mj],
            device_id=dev(yy, ww), device_id_type=MESH,
        )

    def ym_copy(p, o):
        yy, ww = peer(o)
        return pltpu.make_async_remote_copy(
            src_ref=ym_send.at[p, ww * 4 + yy], dst_ref=ym_recv.at[p, mj],
            send_sem=ym_s.at[p, o], recv_sem=ym_r.at[p, mj],
            device_id=dev(yy, ww), device_id_type=MESH,
        )

    def ye_copy(o):
        yy, ww = peer(o)
        return pltpu.make_async_remote_copy(
            src_ref=ye_send.at[ww * 4 + yy], dst_ref=ye_recv.at[mj],
            send_sem=ye_s.at[o], recv_sem=ye_r.at[mj],
            device_id=dev(yy, ww), device_id_type=MESH,
        )

    def project(p):
        got_y(p)
        prod = lax.dot_general(
            wp[...].reshape(2 * PAD, HID), hs[p], (((1,), (1,)), ((), ())),
            preferred_element_type=F32,
        )
        val = jnp.concatenate([prod[0:ROWS], prod[PAD : PAD + ROWS]], axis=0)
        val = val.astype(BF16).astype(F32)
        y_keep[p] = val
        square = jnp.sum(val * val, axis=0, keepdims=True)
        cross = jnp.sum(val * a_keep[p], axis=0, keepdims=True)
        both = jnp.concatenate([square, cross], axis=0)
        st_send[p] = both
        st_recv[p, mj] = both

        @pl.loop(1, 16)
        def _(o):
            st_copy(p, o).start()

        ym_send[p] = val[0:128].T.astype(BF16).reshape(16, 16, 128)
        ext_keep[16 * p : 16 * p + 16, :] = val[128:144]
        ym_recv[p, mj] = ym_send[p, me]

        @pl.loop(1, 16)
        def _(o):
            ym_copy(p, o).start()

    def weights(p, last=False):
        @pl.loop(1, 16)
        def _(o):
            yy, ww = peer(o)
            j = yy * 4 + ww
            arrived(st_recv.at[p, j], st_s.at[p, o], st_r.at[p, j], dev(yy, ww))

        tot = jnp.sum(st_recv[p], axis=0)
        scale = lax.rsqrt(tot[0:1] / D + 1e-06)
        cross = tot[1:2] / D
        dy = (scale * (a_keep[p] - y_keep[p] * (scale * scale * cross))).astype(BF16)
        for k in range(NCH):
            cols = pl.ds(k * CH, CH)
            add = jnp.dot(dy, hs[p, :, cols], preferred_element_type=F32)
            if p == 0:
                grad[:, cols] = add
            else:
                grad[:, cols] += add
            if last:
                other = pl.ds(pl.multiple_of((1 - c) * ROWS, 8), ROWS)
                send(grad.at[other, cols], grad_in.at[:, cols], g_s.at[k], g_r.at[k], dev(y, w, 1 - c))

    relay_z(1)
    spread(1, 1)
    spread(1, 2)
    relay_y(1, 0)
    relay_y(0, 3)
    relay_y(1, 1)
    relay_y(1, 2)
    project(0)

    for k in range(1, 4):
        zz = mod4(zl + k)
        arrived(z_recv.at[zz], dz_s.at[k], dz_r.at[zz], far(x, zz))
    total = z_recv[0].astype(F32) + z_recv[1].astype(F32) + z_recv[2].astype(F32) + z_recv[3].astype(F32)
    o_own[...] = total[0:ROWS]
    o_recv[x] = o_own[...]
    for k in range(1, 4):
        xx = mod4(x + k)
        send(o_own, o_recv.at[x], do_s.at[k], do_r.at[x], far(xx, zl))

    got_z(1)
    spread(1, 3)
    relay_z(2)
    spread(2, 1)
    spread(2, 2)
    relay_y(2, 0)
    relay_y(1, 3)
    relay_y(2, 1)
    relay_y(2, 2)
    weights(0)
    project(1)

    for k in range(1, 4):
        xx = mod4(x + k)
        arrived(o_recv.at[xx], do_s.at[k], do_r.at[xx], far(xx, zl))
    local[6].wait()
    local[7].wait()
    for k in range(4):
        cols = slice(256 * k, 256 * (k + 1))
        average = o_recv[k] / 16.0
        momentum = 0.9 * om[:, cols] + average
        outer_out[:, cols] = op[:, cols] - 0.7 * (average + 0.9 * momentum)

    weights(1)
    got_z(2)
    spread(2, 3)
    relay_y(2, 3)
    project(2)
    ext = jnp.concatenate([ext_keep[...], jnp.zeros((80, TK), F32)], axis=0)
    ye_send[...] = ext.T.astype(BF16).reshape(16, 16, 128)
    ye_recv[mj] = ye_send[me]

    @pl.loop(1, 16)
    def _(o):
        ye_copy(o).start()

    weights(2, last=True)

    local[4].wait()
    local[5].wait()
    mine = pl.ds(pl.multiple_of(c * ROWS, 8), ROWS)
    for k in range(NCH):
        cols = pl.ds(k * CH, CH)
        arrived(grad_in.at[:, cols], g_s.at[k], g_r.at[k], dev(y, w, 1 - c))
        gr = grad[mine, cols] + grad_in[:, cols]
        first = 0.9 * m1[:, cols].astype(F32) + 0.1 * gr
        second = 0.95 * m2[:, cols].astype(F32) + 0.05 * gr * gr
        step = first / (jnp.sqrt(second) + 1e-08) + 0.1 * w_own[:, cols].astype(F32)
        adam_out[:, cols] = step.astype(BF16)

    @pl.loop(1, 16)
    def _(o):
        yy, ww = peer(o)
        j = yy * 4 + ww
        for p in range(PH):
            arrived(ym_recv.at[p, j], ym_s.at[p, o], ym_r.at[p, j], dev(yy, ww))
        arrived(ye_recv.at[j], ye_s.at[o], ye_r.at[j], dev(yy, ww))

    gain = gain_in[...].astype(F32)
    for p in range(PH):
        parts = []
        for j in range(16):
            parts.append(ym_recv[p, j].astype(F32))
            parts.append(ye_recv[j].astype(F32)[:, 16 * p : 16 * p + 16])
        val = jnp.concatenate(parts, axis=1)
        scale = lax.rsqrt(jnp.mean(val * val, axis=1, keepdims=True) + 1e-06)
        norm_out[16 * p : 16 * p + 16, :] = (val * scale * gain).astype(BF16)

    for cp in sent:
        cp.wait_send()

    @pl.loop(1, 16)
    def _(o):
        cot_copy(o).wait_send()
        for p in range(PH):
            st_copy(p, o).wait_send()
            ym_copy(p, o).wait_send()
        ye_copy(o).wait_send()


def per_device(hidden, down_w, m1, m2, gain, cot, delta, outer_params, outer_momentum):
    vm = pl.BlockSpec(memory_space=pltpu.VMEM)
    hbm = pl.BlockSpec(memory_space=pl.ANY)
    dma = pltpu.SemaphoreType.DMA
    scratch = [
        pltpu.VMEM((PH, TK, HID), BF16),
        pltpu.VMEM((2, PAD, HID), BF16),
        pltpu.VMEM((ROWS, HID), BF16),
        pltpu.VMEM((ROWS, HID), BF16),
        pltpu.VMEM((ROWS, HID), BF16),
        pltpu.VMEM((FEAT, HID), F32),
        pltpu.VMEM((ROWS, HID), F32),
        pltpu.VMEM((16, 64, 128), BF16),
        pltpu.VMEM((16, 64, 128), BF16),
        pltpu.VMEM((16, 8, 128), F32),
        pltpu.VMEM((PH, 2, TK), F32),
        pltpu.VMEM((PH, 16, 2, TK), F32),
        pltpu.VMEM((PH, FEAT, TK), F32),
        pltpu.VMEM((PH, FEAT, TK), F32),
        pltpu.VMEM((48, TK), F32),
        pltpu.VMEM((PH, 16, 16, 128), BF16),
        pltpu.VMEM((PH, 16, 16, 128), BF16),
        pltpu.VMEM((16, 16, 128), BF16),
        pltpu.VMEM((16, 16, 128), BF16),
        pltpu.VMEM((4, ROWS, 256), F32),
        pltpu.VMEM((4, ROWS, 256), F32),
        pltpu.VMEM((PAD, 256), BF16),
        pltpu.VMEM((4, PAD, 256), BF16),
        pltpu.VMEM((ROWS, 256), F32),
        pltpu.VMEM((4, ROWS, 256), F32),
        pltpu.VMEM((ROWS, 1024), F32),
        pltpu.VMEM((ROWS, 1024), F32),
        dma((8,)),
        dma((PH, 2)), dma((PH, 2)), dma((PH, 2)), dma((PH, 2)),
        dma((PH, 4, 2)), dma((PH, 4, 2)), dma((PH, 4, 2)), dma((PH, 4, 2)),
        dma((1,)), dma((1,)),
        dma((16,)), dma((16,)),
        dma((PH, 16)), dma((PH, 16)),
        dma((PH, 16)), dma((PH, 16)),
        dma((16,)), dma((16,)),
        dma((NCH,)), dma((NCH,)),
        dma((4,)), dma((4,)), dma((4,)), dma((4,)), dma((4,)), dma((4,)),
    ]
    normed, adam, outer = pl.pallas_call(
        body,
        out_shape=(
            jax.ShapeDtypeStruct((48, D), BF16),
            jax.ShapeDtypeStruct((ROWS, HID), BF16),
            jax.ShapeDtypeStruct((ROWS, 1024), F32),
        ),
        in_specs=[hbm, hbm, hbm, hbm, vm, vm, vm, hbm, hbm],
        out_specs=(vm, vm, vm),
        scratch_shapes=scratch,
        compiler_params=pltpu.CompilerParams(
            collective_id=0, has_side_effects=True, vmem_limit_bytes=50 << 20
        ),
        cost_estimate=pl.CostEstimate(flops=2 * 10**9, bytes_accessed=4 * 10**6, transcendentals=0),
    )(
        hidden, down_w[0], m1[0], m2[0], gain.reshape(1, D), cot, delta[0],
        outer_params, outer_momentum,
    )
    return normed, adam[None], outer


def solution(mesh):
    placed = (
        P(("group", "fsdp"), None),
        P("group", "fsdp", None),
        P("group", "fsdp", None),
        P("group", "fsdp", None),
        P(),
        P(("group", "fsdp"), None),
        P("group", "fsdp", None),
        P("fsdp", None),
        P("fsdp", None),
    )
    return jax.shard_map(
        per_device,
        mesh=mesh,
        in_specs=placed,
        out_specs=(P(("group", "fsdp"), None), P("group", "fsdp", None), P("fsdp", None)),
        check_vma=False,
    )
```

```python
import jax
import jax.numpy as jnp
from jax import lax
from jax.experimental import pallas as pl
from jax.experimental.pallas import tpu as pltpu
from jax.sharding import PartitionSpec as P

MESH = pl.DeviceIdType.MESH
F32 = jnp.float32
BF16 = jnp.bfloat16
D = 2304
HID = 4608
HALF = HID // 2
ROWS = 72
FEAT = 2 * ROWS
PAD = 80
PH = 3
TK = 256
CH = 1152
NCH = HID // CH


def body(
    h_in, w_in, m1_in, m2_in, gain_in, cot_in, delta_in, op_in, om_in,
    norm_hbm, adam_hbm, outer_hbm,
    norm_out, adam_out, outer_out, gain_v,
    hs, wp, w_own, m1, m2, grad, grad_in, cot, delta,
    cot_send, cot_mid, cot_recv, gain_rows, sa_send, sa_recv, sb_send, sb_recv, a_keep, y_keep,
    ra_send, ra_recv, rb_send, rb_recv,
    d_own, d_recv, z_send, z_recv, o_own, o_recv, op, om,
    loc, out_sem, tok_s, zs_r, zx_r, ys_r, yh_r, yx_r,
    w_s, w_r, cot_s, cot_r, all_s, all_r, g_s, g_r,
    dx_s, dx_r, dz_s, dz_r, do_s, do_r,
):
    g = lax.axis_index("group")
    f = lax.axis_index("fsdp")
    x, zl = lax.rem(g, 4), g // 4
    y, w, c = f // 8, lax.rem(f // 2, 4), lax.rem(f, 2)

    def dev(yy, ww, cc=None):
        return (g, yy * 8 + ww * 2 + (c if cc is None else cc))

    def far(xx, zz):
        return (zz * 4 + xx, f)

    def mod4(v):
        return lax.rem(v + 4, 4)

    def peer(o):
        return mod4(y + o // 4), mod4(w + lax.rem(o, 4))

    def rows16(s):
        return pl.ds(pl.multiple_of(s * 16, 16), 16)

    me = w * 4 + y
    mj = y * 4 + w
    yp, ym, wn, wm, wo = mod4(y + 1), mod4(y - 1), mod4(w + 1), mod4(w - 1), mod4(w + 2)
    yo = mod4(y + 2)
    twin = dev(y, w, 1 - c)

    sent, written = [], []

    def put(src, dst, i):
        cp = pltpu.make_async_copy(src, dst, out_sem.at[i])
        cp.start()
        written.append(cp)

    def send(src, dst, s_sem, r_sem, where, keep=True):
        cp = pltpu.make_async_remote_copy(
            src_ref=src, dst_ref=dst, send_sem=s_sem, recv_sem=r_sem,
            device_id=where, device_id_type=MESH,
        )
        cp.start()
        if keep:
            sent.append(cp)

    def arrived(dst, sem):
        pltpu.make_async_copy(dst, dst, sem).wait()

    barrier = pltpu.get_barrier_semaphore()

    @pl.loop(1, 16)
    def _(o):
        pl.semaphore_signal(barrier, inc=1, device_id=dev(*peer(o)), device_id_type=MESH)

    pl.semaphore_signal(barrier, inc=1, device_id=twin, device_id_type=MESH)
    for k in range(1, 4):
        pl.semaphore_signal(barrier, inc=1, device_id=far(mod4(x + k), zl), device_id_type=MESH)
        pl.semaphore_signal(barrier, inc=1, device_id=far(x, mod4(zl + k)), device_id_type=MESH)

    local = [
        pltpu.make_async_copy(src, dst, loc.at[i])
        for i, (src, dst) in enumerate((
            (cot_in, cot), (delta_in, delta), (w_in, w_own),
            (h_in.at[pl.ds(0, 16)], hs.at[0, rows16(me)]),
            (h_in.at[pl.ds(16, 16)], hs.at[1, rows16(me)]),
            (h_in.at[pl.ds(32, 16)], hs.at[2, rows16(me)]),
            (m1_in, m1), (m2_in, m2), (op_in, op), (om_in, om), (gain_in, gain_v),
        ))
    ]
    for cp in local:
        cp.start()

    pl.semaphore_wait(barrier, 22)

    def half(k):
        return pl.ds(k * HALF, HALF)

    def own_z(p):
        src = h_in.at[pl.ds(16 * p, 16)]
        dst = hs.at[p, rows16(me)]
        send(src, dst, tok_s.at[p], zs_r.at[p, 0], dev(y, wn), False)
        send(src, dst, tok_s.at[p], zs_r.at[p, 1], dev(y, wm), False)

    def spread(p, q, src=None):
        dst = hs.at[p, rows16((w, wm, wn)[q] * 4 + y)]
        src = dst if src is None else src
        send(src, dst, tok_s.at[p], ys_r.at[p, q, 0], dev(yp, w), False)
        send(src, dst, tok_s.at[p], ys_r.at[p, q, 1], dev(ym, w), False)

    def relay_z(p):
        for k, (came, to) in enumerate(((wm, wn), (wn, wm))):
            arrived(hs.at[p, rows16(came * 4 + y)], zs_r.at[p, k])
            part = hs.at[p, rows16(came * 4 + y), half(k)]
            send(part, part, tok_s.at[p], zx_r.at[p, k], dev(y, to), False)

    def finish_z(p):
        for k in range(2):
            part = hs.at[p, rows16(wo * 4 + y), half(k)]
            arrived(part, zx_r.at[p, k])
            to, fro = ((yp, ym), (ym, yp))[k]
            send(part, part, tok_s.at[p], yh_r.at[p, k], dev(to, w), False)
            send(part, part, tok_s.at[p], yx_r.at[p], dev(fro, w), False)

    def relay_y(p, q):
        ww = (w, wm, wn)[q]
        for k, (came, to) in enumerate(((ym, yp), (yp, ym))):
            arrived(hs.at[p, rows16(ww * 4 + came)], ys_r.at[p, q, k])
            part = hs.at[p, rows16(ww * 4 + came), half(k)]
            send(part, part, tok_s.at[p], yx_r.at[p], dev(to, w), False)

    def relay_last(p):
        for k, (came, to) in enumerate(((ym, yp), (yp, ym))):
            part = hs.at[p, rows16(wo * 4 + came), half(k)]
            arrived(part, yh_r.at[p, k])
            send(part, part, tok_s.at[p], yx_r.at[p], dev(to, w), False)

    def got_y(p):
        arrived(hs.at[p, pl.ds(0, 80)], yx_r.at[p])

    def cot_y():
        for k in range(1, 4):
            yy = mod4(y + k)
            src = cot_send.at[pl.ds(pl.multiple_of(yy * 4, 4), 4)]
            send(src, cot_mid.at[y], cot_s.at[0], cot_r.at[0], dev(yy, w), False)
        cot_mid[y] = cot_send[pl.ds(pl.multiple_of(y * 4, 4), 4)]

    def cot_z():
        arrived(cot_mid.at[pl.ds(0, 3)], cot_r.at[0])
        here = pl.ds(pl.multiple_of(w * 4, 4), 4)
        for k in (1, 3, 2):
            ww = mod4(w + k)
            send(cot_mid.at[:, ww], cot_recv.at[here], cot_s.at[1], cot_r.at[1], dev(y, ww), False)
        cot_recv[here] = cot_mid[:, w]

    def outer_x():
        local[1].wait()
        d32 = delta[...].astype(F32)
        for k in range(4):
            d_own[k] = d32[:, 256 * k : 256 * (k + 1)]
        for k in range(1, 4):
            xx = mod4(x + k)
            send(d_own.at[xx], d_recv.at[x], dx_s.at[k], dx_r.at[x], far(xx, zl))
        d_recv[x] = d_own[x]

    def outer_z():
        for k in range(1, 4):
            xx = mod4(x + k)
            arrived(d_recv.at[xx], dx_r.at[xx])
        part_x = d_recv[0] + d_recv[1] + d_recv[2] + d_recv[3]
        z_send[...] = jnp.concatenate([part_x, jnp.zeros((PAD - ROWS, 256), F32)], axis=0).astype(BF16)
        z_recv[zl] = z_send[...]
        for k in range(1, 4):
            zz = mod4(zl + k)
            send(z_send, z_recv.at[zl], dz_s.at[k], dz_r.at[zl], far(x, zz))

    def outer_back():
        for k in range(1, 4):
            zz = mod4(zl + k)
            arrived(z_recv.at[zz], dz_r.at[zz])
        total = z_recv[0].astype(F32) + z_recv[1].astype(F32) + z_recv[2].astype(F32) + z_recv[3].astype(F32)
        o_own[...] = total[0:ROWS]
        o_recv[x] = o_own[...]
        for k in range(1, 4):
            xx = mod4(x + k)
            send(o_own, o_recv.at[x], do_s.at[k], do_r.at[x], far(xx, zl))

    def outer_step():
        for k in range(1, 4):
            xx = mod4(x + k)
            arrived(o_recv.at[xx], do_r.at[xx])
        local[8].wait()
        local[9].wait()
        for k in range(4):
            cols = slice(256 * k, 256 * (k + 1))
            average = o_recv[k] / 16.0
            momentum = 0.9 * om[:, cols] + average
            outer_out[:, cols] = op[:, cols] - 0.7 * (average + 0.9 * momentum)
        put(outer_out, outer_hbm, 0)

    def share_w():
        local[2].wait()
        w32 = w_own[...].astype(F32)
        wp[c] = jnp.concatenate([w32, jnp.zeros((PAD - ROWS, HID), F32)], axis=0).astype(BF16)
        send(wp.at[c], wp.at[c], w_s.at[0], w_r.at[0], twin)

    def pack_cot():
        zero = jnp.zeros((16, 80), F32)
        local[0].wait()
        local[10].wait()
        gain = gain_v[...].reshape(1, D).astype(F32)
        for j in range(16):
            part = cot[:, FEAT * j : FEAT * (j + 1)].astype(F32)
            tail = part[:, 128:]
            tail = jnp.concatenate([tail[0:16], tail[16:32], tail[32:48], zero], axis=1)
            cot_send[j] = jnp.concatenate([part[:, :128], tail], axis=0).astype(BF16)
            gj = gain[:, FEAT * j : FEAT * (j + 1)]
            gain_rows[j, 0:1, :] = gj[:, :128]
            gain_rows[j, 1:2, :] = jnp.concatenate([gj[:, 128:], jnp.zeros((1, 112), F32)], axis=1)

    def own(p):
        spread(p, 0, h_in.at[pl.ds(16 * p, 16)])

    def ready():
        arrived(wp.at[1 - c], w_r.at[0])
        local[3].wait()
        local[4].wait()
        local[5].wait()

    def get_cot():
        arrived(cot_recv.at[pl.ds(0, 12)], cot_r.at[1])

        gt = gain_rows[mj]
        gmain = jnp.broadcast_to(gt[0:1, :], (128, 128)).T
        gext = jnp.broadcast_to(gt[1:2, :], (128, 128)).T
        gcol = jnp.concatenate([gmain, gext[0:16]], axis=0)
        gcol = jnp.concatenate([gcol, gcol], axis=1)
        ext_all = cot_recv[:, 48:64, :].reshape(TK, 128).astype(F32).T
        for p in range(PH):
            main = cot_recv[:, 16 * p : 16 * p + 16, :].reshape(TK, 128).astype(F32).T
            a_keep[p] = gcol * jnp.concatenate([main, ext_all[16 * p : 16 * p + 16]], axis=0)

    def sums_a():
        both = jnp.concatenate([sums(0), sums(1)], axis=1)
        sa_send[...] = both
        sa_recv[mj] = both

    def sums_b():
        both = sums(2)
        sb_send[...] = both
        sb_recv[mj] = both

    def weights_a():
        got_all(sa_recv, 0)

        tot = jnp.sum(sa_recv[...], axis=0)
        weights(0, tot[:, 0:TK])
        weights(1, tot[:, TK : 2 * TK])

    def get_b():
        got_all(sb_recv, 1)

    def weights_b():
        weights(2, jnp.sum(sb_recv[...], axis=0), last=True)

    def swapped(k):
        cols = pl.ds(k * CH, CH)
        arrived(grad_in.at[:, cols], g_r.at[k])

    def adam(k):
        mine = pl.ds(pl.multiple_of(c * ROWS, 8), ROWS)
        cols = pl.ds(k * CH, CH)
        gr = grad[mine, cols] + grad_in[:, cols]
        first = 0.9 * m1[:, cols].astype(F32) + 0.1 * gr
        second = 0.95 * m2[:, cols].astype(F32) + 0.05 * gr * gr
        step = first / (jnp.sqrt(second) + 1e-08) + 0.1 * w_own[:, cols].astype(F32)
        adam_out[:, cols] = step.astype(BF16)
        put(adam_out.at[:, cols], adam_hbm.at[:, cols], 2 + k)

    def moments():
        local[6].wait()
        local[7].wait()

    def get_ret():
        got_all(ra_recv, 2)
        got_all(rb_recv, 3)

    def norm_rows():
        gain = gain_v[...].reshape(1, D).astype(F32)
        for p in range(PH):
            parts = []
            for j in range(16):
                main = ra_recv[j, 16 * p : 16 * p + 16, :] if p < 2 else rb_recv[j, 0:16, :]
                parts.append(main.astype(F32))
                parts.append(rb_recv[j, 16:32, :].astype(F32)[:, 16 * p : 16 * p + 16])
            val = jnp.concatenate(parts, axis=1)
            scale = lax.rsqrt(jnp.mean(val * val, axis=1, keepdims=True) + 1e-06)
            norm_out[16 * p : 16 * p + 16, :] = (val * scale * gain).astype(BF16)
        put(norm_out, norm_hbm, 1)

    def drain():
        for cp in written:
            cp.wait()
        for cp in sent:
            cp.wait_send()
        for p in range(PH):
            arrived(hs.at[p, pl.ds(0, 240)], tok_s.at[p])
        arrived(cot_mid.at[pl.ds(0, 3)], cot_s.at[0])
        arrived(cot_recv.at[pl.ds(0, 12)], cot_s.at[1])
        for i, ref in enumerate((sa_recv, sb_recv, ra_recv, rb_recv)):
            arrived(ref.at[pl.ds(0, 15)], all_s.at[i])

    def to_peer(o, src, dst, i):
        yy, ww = peer(o)
        return pltpu.make_async_remote_copy(
            src_ref=src(yy, ww), dst_ref=dst, send_sem=all_s.at[i], recv_sem=all_r.at[i],
            device_id=dev(yy, ww), device_id_type=MESH,
        )

    def sa_copy(o):
        return to_peer(o, lambda yy, ww: sa_send, sa_recv.at[mj], 0)

    def sb_copy(o):
        return to_peer(o, lambda yy, ww: sb_send, sb_recv.at[mj], 1)

    def ra_copy(o):
        return to_peer(o, lambda yy, ww: ra_send.at[ww * 4 + yy], ra_recv.at[mj], 2)

    def rb_copy(o):
        return to_peer(o, lambda yy, ww: rb_send.at[ww * 4 + yy], rb_recv.at[mj], 3)

    def got_all(ref, i):
        arrived(ref.at[pl.ds(0, 15)], all_r.at[i])

    def start_all(copy):
        @pl.loop(1, 16)
        def _(o):
            copy(o).start()

    def project(p):
        got_y(p)
        prod = lax.dot_general(
            wp[...].reshape(2 * PAD, HID), hs[p], (((1,), (1,)), ((), ())),
            preferred_element_type=F32,
        )
        val = jnp.concatenate([prod[0:ROWS], prod[PAD : PAD + ROWS]], axis=0)
        y_keep[p] = val.astype(BF16).astype(F32)

    def pack_a():
        for p in range(2):
            val = y_keep[p]
            ra_send[:, 16 * p : 16 * p + 16, :] = val[0:128].T.astype(BF16).reshape(16, 16, 128)
        ra_recv[mj] = ra_send[me]

    def pack_b():
        val = y_keep[2]
        rb_send[:, 0:16, :] = val[0:128].T.astype(BF16).reshape(16, 16, 128)
        ext = [y_keep[p][128:144] for p in range(PH)]
        ext = jnp.concatenate(ext + [jnp.zeros((80, TK), F32)], axis=0)
        rb_send[:, 16:32, :] = ext.T.astype(BF16).reshape(16, 16, 128)
        rb_recv[mj] = rb_send[me]

    def sums(p):
        val = y_keep[p]
        square = jnp.sum(val * val, axis=0, keepdims=True)
        cross = jnp.sum(val * a_keep[p], axis=0, keepdims=True)
        return jnp.concatenate([square, cross], axis=0)

    def weights(p, tot, last=False):
        scale = lax.rsqrt(tot[0:1] / D + 1e-06)
        cross = tot[1:2] / D
        dy = (scale * (a_keep[p] - y_keep[p] * (scale * scale * cross))).astype(BF16)
        for k in range(NCH):
            cols = pl.ds(k * CH, CH)
            add = jnp.dot(dy, hs[p, :, cols], preferred_element_type=F32)
            if p == 0:
                grad[:, cols] = add
            else:
                grad[:, cols] += add
            if last:
                other = pl.ds(pl.multiple_of((1 - c) * ROWS, 8), ROWS)
                send(grad.at[other, cols], grad_in.at[:, cols], g_s.at[k], g_r.at[k], twin)

    own_z(0)
    own(0)
    own_z(1)
    own(1)
    own(2)
    outer_x()
    share_w()
    pack_cot()
    cot_y()
    relay_y(0, 0)
    own_z(2)
    relay_y(1, 0)
    relay_y(2, 0)
    relay_z(0)
    spread(0, 1)
    spread(0, 2)
    outer_z()
    relay_y(0, 1)
    relay_y(0, 2)
    relay_z(1)
    spread(1, 1)
    spread(1, 2)
    relay_y(1, 1)
    relay_y(1, 2)
    relay_z(2)
    spread(2, 1)
    spread(2, 2)
    finish_z(0)
    relay_y(2, 1)
    relay_y(2, 2)
    relay_last(0)
    finish_z(1)
    cot_z()
    relay_last(1)
    ready()
    project(0)
    finish_z(2)
    relay_last(2)
    project(1)
    outer_back()
    get_cot()
    sums_a()
    start_all(sa_copy)
    pack_a()
    start_all(ra_copy)
    outer_step()
    project(2)
    sums_b()
    start_all(sb_copy)
    pack_b()
    start_all(rb_copy)
    weights_a()
    moments()
    get_b()
    weights_b()
    for k in range(NCH):
        swapped(k)
        adam(k)
    get_ret()
    norm_rows()
    drain()


def place_body(a_in, b_in, c_in, a_out, b_out, c_out, a, b, c, sem):
    stages = ((a_in, a, a_out), (b_in, b, b_out), (c_in, c, c_out))
    loads = [pltpu.make_async_copy(src, mid, sem.at[i]) for i, (src, mid, _) in enumerate(stages)]
    stores = [pltpu.make_async_copy(mid, dst, sem.at[3 + i]) for i, (_, mid, dst) in enumerate(stages)]
    for cp in loads:
        cp.start()
    for load, store in zip(loads, stores):
        load.wait()
        store.start()
    for cp in stores:
        cp.wait()


def place(*arrays):
    hbm = pl.BlockSpec(memory_space=pl.ANY)
    return pl.pallas_call(
        place_body,
        out_shape=tuple(jax.ShapeDtypeStruct(a.shape, a.dtype) for a in arrays),
        in_specs=[hbm] * 3,
        out_specs=(hbm,) * 3,
        scratch_shapes=[pltpu.VMEM(a.shape, a.dtype) for a in arrays] + [pltpu.SemaphoreType.DMA((6,))],
        compiler_params=pltpu.CompilerParams(vmem_limit_bytes=63 << 20),
    )(*arrays)


def per_device(hidden, down_w, m1, m2, gain, cot, delta, outer_params, outer_momentum):
    hbm = pl.BlockSpec(memory_space=pl.ANY)
    dma = pltpu.SemaphoreType.DMA
    scratch = [
        pltpu.VMEM((48, D), BF16),
        pltpu.VMEM((ROWS, HID), BF16),
        pltpu.VMEM((ROWS, 1024), F32),
        pltpu.VMEM((D,), BF16),
        pltpu.VMEM((PH, TK, HID), BF16),
        pltpu.VMEM((2, PAD, HID), BF16),
        pltpu.VMEM((ROWS, HID), BF16),
        pltpu.VMEM((ROWS, HID), BF16),
        pltpu.VMEM((ROWS, HID), BF16),
        pltpu.VMEM((FEAT, HID), F32),
        pltpu.VMEM((ROWS, HID), F32),
        pltpu.VMEM((48, D), BF16),
        pltpu.VMEM((ROWS, 1024), BF16),
        pltpu.VMEM((16, 64, 128), BF16),
        pltpu.VMEM((4, 4, 64, 128), BF16),
        pltpu.VMEM((16, 64, 128), BF16),
        pltpu.VMEM((16, 8, 128), F32),
        pltpu.VMEM((2, 2 * TK), F32),
        pltpu.VMEM((16, 2, 2 * TK), F32),
        pltpu.VMEM((2, TK), F32),
        pltpu.VMEM((16, 2, TK), F32),
        pltpu.VMEM((PH, FEAT, TK), F32),
        pltpu.VMEM((PH, FEAT, TK), F32),
        pltpu.VMEM((16, 32, 128), BF16),
        pltpu.VMEM((16, 32, 128), BF16),
        pltpu.VMEM((16, 32, 128), BF16),
        pltpu.VMEM((16, 32, 128), BF16),
        pltpu.VMEM((4, ROWS, 256), F32),
        pltpu.VMEM((4, ROWS, 256), F32),
        pltpu.VMEM((PAD, 256), BF16),
        pltpu.VMEM((4, PAD, 256), BF16),
        pltpu.VMEM((ROWS, 256), F32),
        pltpu.VMEM((4, ROWS, 256), F32),
        pltpu.VMEM((ROWS, 1024), F32),
        pltpu.VMEM((ROWS, 1024), F32),
        dma((11,)), dma((2 + NCH,)),
        dma((PH,)), dma((PH, 2)), dma((PH, 2)), dma((PH, 3, 2)), dma((PH, 2)), dma((PH,)),
        dma((1,)), dma((1,)),
        dma((2,)), dma((2,)), dma((4,)), dma((4,)),
        dma((NCH,)), dma((NCH,)),
        dma((4,)), dma((4,)), dma((4,)), dma((4,)), dma((4,)), dma((4,)),
    ]
    normed, adam, outer = pl.pallas_call(
        body,
        out_shape=(
            jax.ShapeDtypeStruct((48, D), BF16),
            jax.ShapeDtypeStruct((ROWS, HID), BF16),
            jax.ShapeDtypeStruct((ROWS, 1024), F32),
        ),
        in_specs=[hbm] * 9,
        out_specs=(hbm, hbm, hbm),
        scratch_shapes=scratch,
        compiler_params=pltpu.CompilerParams(
            collective_id=0, has_side_effects=True, vmem_limit_bytes=63 << 20
        ),
        cost_estimate=pl.CostEstimate(flops=2 * 10**9, bytes_accessed=4 * 10**6, transcendentals=0),
    )(
        hidden, down_w[0], m1[0], m2[0], gain, cot, delta[0],
        outer_params, outer_momentum,
    )
    return place(normed, adam[None], outer)


def solution(mesh):
    placed = (
        P(("group", "fsdp"), None),
        P("group", "fsdp", None),
        P("group", "fsdp", None),
        P("group", "fsdp", None),
        P(),
        P(("group", "fsdp"), None),
        P("group", "fsdp", None),
        P("fsdp", None),
        P("fsdp", None),
    )
    return jax.shard_map(
        per_device,
        mesh=mesh,
        in_specs=placed,
        out_specs=(P(("group", "fsdp"), None), P("group", "fsdp", None), P("fsdp", None)),
        check_vma=False,
    )
```

```python
import jax
import jax.numpy as jnp
from jax import lax
from jax.experimental import pallas as pl
from jax.experimental.pallas import tpu as pltpu
from jax.sharding import PartitionSpec as P

MESH = pl.DeviceIdType.MESH
F32 = jnp.float32
BF16 = jnp.bfloat16
D = 2304
HID = 4608
HALF = HID // 2
ROWS = 72
FEAT = 2 * ROWS
PAD = 80
PH = 3
TK = 256
CH = 1536
NCH = HID // CH


def body(
    h_in, w_in, m1_in, m2_in, gain_in, cot_in, delta_in, op_in, om_in,
    norm_hbm, adam_hbm, outer_hbm,
    norm_out, adam_out, outer_out, gain_v,
    hs, wp, wt, w_own, m1, m2, grad, grad_in, cot, delta,
    cot_send, cot_mid, cot_recv, gain_rows, st_send, st_mid, st_y, st_z, a_keep, y_keep,
    ra_send, ra_recv, rb_send, rb_recv,
    d_own, d_recv, z_send, z_recv, o_own, o_recv, op, om,
    loc, out_sem, tok_s, zs_r, zx_r, ys_r, yh_r, yx_r,
    w_s, w_r, cot_s, cot_r, st_s, st_r, all_s, all_r, g_s, g_r,
    dx_s, dx_r, dz_s, dz_r, do_s, do_r,
):
    g = lax.axis_index("group")
    f = lax.axis_index("fsdp")
    x, zl = lax.rem(g, 4), g // 4
    y, w, c = f // 8, lax.rem(f // 2, 4), lax.rem(f, 2)

    def dev(yy, ww, cc=None):
        return (g, yy * 8 + ww * 2 + (c if cc is None else cc))

    def far(xx, zz):
        return (zz * 4 + xx, f)

    def mod4(v):
        return lax.rem(v + 4, 4)

    def peer(o):
        return mod4(y + o // 4), mod4(w + lax.rem(o, 4))

    def rows16(s):
        return pl.ds(pl.multiple_of(s * 16, 16), 16)

    me = w * 4 + y
    mj = y * 4 + w
    yp, ym, wn, wm, wo = mod4(y + 1), mod4(y - 1), mod4(w + 1), mod4(w - 1), mod4(w + 2)
    yo = mod4(y + 2)
    twin = dev(y, w, 1 - c)

    sent, written = [], []

    def put(src, dst, i):
        cp = pltpu.make_async_copy(src, dst, out_sem.at[i])
        cp.start()
        written.append(cp)

    def send(src, dst, s_sem, r_sem, where, keep=True):
        cp = pltpu.make_async_remote_copy(
            src_ref=src, dst_ref=dst, send_sem=s_sem, recv_sem=r_sem,
            device_id=where, device_id_type=MESH,
        )
        cp.start()
        if keep:
            sent.append(cp)

    def arrived(dst, sem):
        pltpu.make_async_copy(dst, dst, sem).wait()

    barrier = pltpu.get_barrier_semaphore()

    @pl.loop(1, 16)
    def _(o):
        pl.semaphore_signal(barrier, inc=1, device_id=dev(*peer(o)), device_id_type=MESH)

    pl.semaphore_signal(barrier, inc=1, device_id=twin, device_id_type=MESH)
    for k in range(1, 4):
        pl.semaphore_signal(barrier, inc=1, device_id=far(mod4(x + k), zl), device_id_type=MESH)
        pl.semaphore_signal(barrier, inc=1, device_id=far(x, mod4(zl + k)), device_id_type=MESH)

    local = [
        pltpu.make_async_copy(src, dst, loc.at[i])
        for i, (src, dst) in enumerate((
            (cot_in, cot), (delta_in, delta), (w_in, w_own),
            (h_in.at[pl.ds(0, 16)], hs.at[0, rows16(me)]),
            (h_in.at[pl.ds(16, 16)], hs.at[1, rows16(me)]),
            (h_in.at[pl.ds(32, 16)], hs.at[2, rows16(me)]),
            (m1_in, m1), (m2_in, m2), (op_in, op), (om_in, om), (gain_in, gain_v),
        ))
    ]
    for cp in local:
        cp.start()

    pl.semaphore_wait(barrier, 22)

    def half(k):
        return pl.ds(k * HALF, HALF)

    def own_z(p):
        src = h_in.at[pl.ds(16 * p, 16)]
        dst = hs.at[p, rows16(me)]
        send(src, dst, tok_s.at[p], zs_r.at[p, 0], dev(y, wn), False)
        send(src, dst, tok_s.at[p], zs_r.at[p, 1], dev(y, wm), False)

    def spread(p, q, src=None):
        dst = hs.at[p, rows16((w, wm, wn)[q] * 4 + y)]
        src = dst if src is None else src
        send(src, dst, tok_s.at[p], ys_r.at[p, q, 0], dev(yp, w), False)
        send(src, dst, tok_s.at[p], ys_r.at[p, q, 1], dev(ym, w), False)

    def relay_z(p):
        for k, (came, to) in enumerate(((wm, wn), (wn, wm))):
            arrived(hs.at[p, rows16(came * 4 + y)], zs_r.at[p, k])
            part = hs.at[p, rows16(came * 4 + y), half(k)]
            send(part, part, tok_s.at[p], zx_r.at[p, k], dev(y, to), False)

    def finish_z(p):
        for k in range(2):
            part = hs.at[p, rows16(wo * 4 + y), half(k)]
            arrived(part, zx_r.at[p, k])
            to, fro = ((yp, ym), (ym, yp))[k]
            send(part, part, tok_s.at[p], yh_r.at[p, k], dev(to, w), False)
            send(part, part, tok_s.at[p], yx_r.at[p], dev(fro, w), False)

    def relay_y(p, q):
        ww = (w, wm, wn)[q]
        for k, (came, to) in enumerate(((ym, yp), (yp, ym))):
            arrived(hs.at[p, rows16(ww * 4 + came)], ys_r.at[p, q, k])
            part = hs.at[p, rows16(ww * 4 + came), half(k)]
            send(part, part, tok_s.at[p], yx_r.at[p], dev(to, w), False)

    def relay_last(p):
        for k, (came, to) in enumerate(((ym, yp), (yp, ym))):
            part = hs.at[p, rows16(wo * 4 + came), half(k)]
            arrived(part, yh_r.at[p, k])
            send(part, part, tok_s.at[p], yx_r.at[p], dev(to, w), False)

    def got_y(p):
        arrived(hs.at[p, pl.ds(0, 80)], yx_r.at[p])

    def cot_y():
        for k in range(1, 4):
            yy = mod4(y + k)
            src = cot_send.at[pl.ds(pl.multiple_of(yy * 4, 4), 4)]
            send(src, cot_mid.at[y], cot_s.at[0], cot_r.at[0], dev(yy, w), False)
        cot_mid[y] = cot_send[pl.ds(pl.multiple_of(y * 4, 4), 4)]

    def cot_z():
        arrived(cot_mid.at[pl.ds(0, 3)], cot_r.at[0])
        here = pl.ds(pl.multiple_of(w * 4, 4), 4)
        for k in (2, 1, 3):
            ww = mod4(w + k)
            send(cot_mid.at[:, ww], cot_recv.at[here], cot_s.at[1], cot_r.at[1], dev(y, ww), False)
        cot_recv[here] = cot_mid[:, w]

    def outer_x():
        local[1].wait()
        d32 = delta[...].astype(F32)
        for k in range(4):
            d_own[k] = d32[:, 256 * k : 256 * (k + 1)]
        for k in range(1, 4):
            xx = mod4(x + k)
            send(d_own.at[xx], d_recv.at[x], dx_s.at[k], dx_r.at[x], far(xx, zl))
        d_recv[x] = d_own[x]

    def outer_z():
        for k in range(1, 4):
            xx = mod4(x + k)
            arrived(d_recv.at[xx], dx_r.at[xx])
        part_x = d_recv[0] + d_recv[1] + d_recv[2] + d_recv[3]
        z_send[...] = jnp.concatenate([part_x, jnp.zeros((PAD - ROWS, 256), F32)], axis=0).astype(BF16)
        z_recv[zl] = z_send[...]
        for k in range(1, 4):
            zz = mod4(zl + k)
            send(z_send, z_recv.at[zl], dz_s.at[k], dz_r.at[zl], far(x, zz))

    def outer_back():
        for k in range(1, 4):
            zz = mod4(zl + k)
            arrived(z_recv.at[zz], dz_r.at[zz])
        total = z_recv[0].astype(F32) + z_recv[1].astype(F32) + z_recv[2].astype(F32) + z_recv[3].astype(F32)
        o_own[...] = total[0:ROWS]
        o_recv[x] = o_own[...]
        for k in range(1, 4):
            xx = mod4(x + k)
            send(o_own, o_recv.at[x], do_s.at[k], do_r.at[x], far(xx, zl))

    def outer_step():
        for k in range(1, 4):
            xx = mod4(x + k)
            arrived(o_recv.at[xx], do_r.at[xx])
        local[8].wait()
        local[9].wait()
        for k in range(4):
            cols = slice(256 * k, 256 * (k + 1))
            average = o_recv[k] / 16.0
            momentum = 0.9 * om[:, cols] + average
            outer_out[:, cols] = op[:, cols] - 0.7 * (average + 0.9 * momentum)
        put(outer_out, outer_hbm, 0)

    def share_w():
        local[2].wait()
        w32 = w_own[...].astype(F32)
        wp[c] = jnp.concatenate([w32, jnp.zeros((PAD - ROWS, HID), F32)], axis=0).astype(BF16)
        send(wp.at[c], wp.at[c], w_s.at[0], w_r.at[0], twin)

    def pack_cot():
        zero = jnp.zeros((16, 80), F32)
        local[0].wait()
        local[10].wait()
        gain = gain_v[...].reshape(1, D).astype(F32)
        for j in range(16):
            part = cot[:, FEAT * j : FEAT * (j + 1)].astype(F32)
            tail = part[:, 128:]
            tail = jnp.concatenate([tail[0:16], tail[16:32], tail[32:48], zero], axis=1)
            cot_send[j] = jnp.concatenate([part[:, :128], tail], axis=0).astype(BF16)
            gj = gain[:, FEAT * j : FEAT * (j + 1)]
            gain_rows[j, 0:1, :] = gj[:, :128]
            gain_rows[j, 1:2, :] = jnp.concatenate([gj[:, 128:], jnp.zeros((1, 112), F32)], axis=1)

    def own(p):
        spread(p, 0, h_in.at[pl.ds(16 * p, 16)])

    def ready():
        arrived(wp.at[1 - c], w_r.at[0])
        for k in range(NCH):
            cols = pl.ds(k * CH, CH)
            part = wp[:, :, cols].reshape(2 * PAD, CH).astype(F32).T
            wt[cols, :] = part.astype(BF16)
        local[3].wait()
        local[4].wait()
        local[5].wait()

    def get_cot():
        arrived(cot_recv.at[pl.ds(0, 12)], cot_r.at[1])

        gt = gain_rows[mj]
        gmain = jnp.broadcast_to(gt[0:1, :], (128, 128)).T
        gext = jnp.broadcast_to(gt[1:2, :], (128, 128)).T
        gcol = jnp.concatenate([gmain, gext[0:16]], axis=0)
        gcol = jnp.concatenate([gcol, gcol], axis=1)
        ext_all = cot_recv[:, 48:64, :].reshape(TK, 128).astype(F32).T
        for p in range(PH):
            main = cot_recv[:, 16 * p : 16 * p + 16, :].reshape(TK, 128).astype(F32).T
            a_keep[:, TK * p : TK * (p + 1)] = gcol * jnp.concatenate([main, ext_all[16 * p : 16 * p + 16]], axis=0)

    def sums_y():
        arrived(st_y.at[pl.ds(0, 3)], st_r.at[0])
        both = jnp.sum(st_y[...], axis=0)
        st_mid[...] = both
        st_z[w] = both
        for k in (2, 1, 3):
            send(st_mid, st_z.at[w], st_s.at[1], st_r.at[1], dev(y, mod4(w + k)), False)

    def get_stats():
        arrived(st_z.at[pl.ds(0, 3)], st_r.at[1])

    def swapped(k):
        cols = pl.ds(k * CH, CH)
        arrived(grad_in.at[:, cols], g_r.at[k])

    def adam(k):
        mine = pl.ds(pl.multiple_of(c * ROWS, 8), ROWS)
        cols = pl.ds(k * CH, CH)
        gr = grad[mine, cols] + grad_in[:, cols]
        first = 0.9 * m1[:, cols].astype(F32) + 0.1 * gr
        second = 0.95 * m2[:, cols].astype(F32) + 0.05 * gr * gr
        step = first / (jnp.sqrt(second) + 1e-08) + 0.1 * w_own[:, cols].astype(F32)
        adam_out[:, cols] = step.astype(BF16)
        put(adam_out.at[:, cols], adam_hbm.at[:, cols], 2 + k)

    def moments():
        local[6].wait()
        local[7].wait()

    def get_ret():
        got_all(ra_recv, 0)
        got_all(rb_recv, 1)

    def norm_rows():
        gain = gain_v[...].reshape(1, D).astype(F32)
        for p in range(PH):
            parts = []
            for j in range(16):
                main = ra_recv[j, 16 * p : 16 * p + 16, :] if p < 2 else rb_recv[j, 0:16, :]
                parts.append(main.astype(F32))
                parts.append(rb_recv[j, 16:32, :].astype(F32)[:, 16 * p : 16 * p + 16])
            val = jnp.concatenate(parts, axis=1)
            scale = lax.rsqrt(jnp.mean(val * val, axis=1, keepdims=True) + 1e-06)
            norm_out[16 * p : 16 * p + 16, :] = (val * scale * gain).astype(BF16)
        put(norm_out, norm_hbm, 1)

    def drain():
        for cp in written:
            cp.wait()
        for cp in sent:
            cp.wait_send()
        for p in range(PH):
            arrived(hs.at[p, pl.ds(0, 240)], tok_s.at[p])
        arrived(cot_mid.at[pl.ds(0, 3)], cot_s.at[0])
        arrived(cot_recv.at[pl.ds(0, 12)], cot_s.at[1])
        for i in range(2):
            arrived(st_y.at[pl.ds(0, 3)], st_s.at[i])
        for i, ref in enumerate((ra_recv, rb_recv)):
            arrived(ref.at[pl.ds(0, 15)], all_s.at[i])

    def to_peer(o, src, dst, i):
        yy, ww = peer(o)
        return pltpu.make_async_remote_copy(
            src_ref=src(yy, ww), dst_ref=dst, send_sem=all_s.at[i], recv_sem=all_r.at[i],
            device_id=dev(yy, ww), device_id_type=MESH,
        )

    def ra_copy(o):
        return to_peer(o, lambda yy, ww: ra_send.at[ww * 4 + yy], ra_recv.at[mj], 0)

    def rb_copy(o):
        return to_peer(o, lambda yy, ww: rb_send.at[ww * 4 + yy], rb_recv.at[mj], 1)

    def got_all(ref, i):
        arrived(ref.at[pl.ds(0, 15)], all_r.at[i])

    def start_all(copy):
        @pl.loop(1, 16)
        def _(o):
            copy(o).start()

    def project(p):
        got_y(p)
        prod = jnp.dot(hs[p], wt[...], preferred_element_type=F32).T
        val = jnp.concatenate([prod[0:ROWS], prod[PAD : PAD + ROWS]], axis=0)
        y_keep[:, TK * p : TK * (p + 1)] = val.astype(BF16).astype(F32)

    def pack_a():
        for p in range(2):
            val = y_keep[:, TK * p : TK * (p + 1)]
            ra_send[:, 16 * p : 16 * p + 16, :] = val[0:128].T.astype(BF16).reshape(16, 16, 128)
        ra_recv[mj] = ra_send[me]

    def pack_b():
        val = y_keep[:, 2 * TK :]
        rb_send[:, 0:16, :] = val[0:128].T.astype(BF16).reshape(16, 16, 128)
        ext = [y_keep[128:144, TK * p : TK * (p + 1)] for p in range(PH)]
        ext = jnp.concatenate(ext + [jnp.zeros((80, TK), F32)], axis=0)
        rb_send[:, 16:32, :] = ext.T.astype(BF16).reshape(16, 16, 128)
        rb_recv[mj] = rb_send[me]

    def sums():
        val = y_keep[...]
        square = jnp.sum(val * val, axis=0, keepdims=True)
        cross = jnp.sum(val * a_keep[...], axis=0, keepdims=True)
        both = jnp.concatenate([square, cross], axis=0)
        st_send[...] = both
        st_y[y] = both
        for k in range(1, 4):
            send(st_send, st_y.at[y], st_s.at[0], st_r.at[0], dev(mod4(y + k), w), False)

    def weights():
        tot = jnp.sum(st_z[...], axis=0)
        scale = lax.rsqrt(tot[0:1] / D + 1e-06)
        cross = tot[1:2] / D
        dy = (scale * (a_keep[...] - y_keep[...] * (scale * scale * cross))).astype(BF16)
        other = pl.ds(pl.multiple_of((1 - c) * ROWS, 8), ROWS)
        for k in range(NCH):
            cols = pl.ds(k * CH, CH)
            grad[:, cols] = jnp.dot(
                dy, hs[:, :, cols].reshape(PH * TK, CH), preferred_element_type=F32
            )
            send(grad.at[other, cols], grad_in.at[:, cols], g_s.at[k], g_r.at[k], twin)

    own_z(0)
    own(0)
    own_z(1)
    own(1)
    own(2)
    outer_x()
    share_w()
    pack_cot()
    cot_y()
    relay_y(0, 0)
    own_z(2)
    relay_y(1, 0)
    relay_y(2, 0)
    relay_z(0)
    spread(0, 1)
    spread(0, 2)
    outer_z()
    relay_y(0, 1)
    relay_y(0, 2)
    relay_z(1)
    spread(1, 1)
    spread(1, 2)
    relay_y(1, 1)
    relay_z(2)
    spread(2, 1)
    spread(2, 2)
    relay_y(1, 2)
    finish_z(0)
    relay_y(2, 1)
    relay_y(2, 2)
    relay_last(0)
    ready()
    finish_z(1)
    cot_z()
    finish_z(2)
    relay_last(1)
    outer_back()
    project(0)
    relay_last(2)
    project(1)
    pack_a()
    start_all(ra_copy)
    get_cot()
    project(2)
    sums()
    pack_b()
    moments()
    outer_step()
    sums_y()
    start_all(rb_copy)
    get_stats()
    weights()
    for k in range(NCH):
        swapped(k)
        adam(k)
    get_ret()
    norm_rows()
    drain()


def place_body(a_in, b_in, c_in, a_out, b_out, c_out, a, b, c, sem):
    stages = ((a_in, a, a_out), (b_in, b, b_out), (c_in, c, c_out))
    loads = [pltpu.make_async_copy(src, mid, sem.at[i]) for i, (src, mid, _) in enumerate(stages)]
    stores = [pltpu.make_async_copy(mid, dst, sem.at[3 + i]) for i, (_, mid, dst) in enumerate(stages)]
    for cp in loads:
        cp.start()
    for load, store in zip(loads, stores):
        load.wait()
        store.start()
    for cp in stores:
        cp.wait()


def place(*arrays):
    hbm = pl.BlockSpec(memory_space=pl.ANY)
    return pl.pallas_call(
        place_body,
        out_shape=tuple(jax.ShapeDtypeStruct(a.shape, a.dtype) for a in arrays),
        in_specs=[hbm] * 3,
        out_specs=(hbm,) * 3,
        scratch_shapes=[pltpu.VMEM(a.shape, a.dtype) for a in arrays] + [pltpu.SemaphoreType.DMA((6,))],
        compiler_params=pltpu.CompilerParams(vmem_limit_bytes=63 << 20),
    )(*arrays)


def per_device(hidden, down_w, m1, m2, gain, cot, delta, outer_params, outer_momentum):
    hbm = pl.BlockSpec(memory_space=pl.ANY)
    dma = pltpu.SemaphoreType.DMA
    scratch = [
        pltpu.VMEM((48, D), BF16),
        pltpu.VMEM((ROWS, HID), BF16),
        pltpu.VMEM((ROWS, 1024), F32),
        pltpu.VMEM((D,), BF16),
        pltpu.VMEM((PH, TK, HID), BF16),
        pltpu.VMEM((2, PAD, HID), BF16),
        pltpu.VMEM((HID, 2 * PAD), BF16),
        pltpu.VMEM((ROWS, HID), BF16),
        pltpu.VMEM((ROWS, HID), BF16),
        pltpu.VMEM((ROWS, HID), BF16),
        pltpu.VMEM((FEAT, HID), F32),
        pltpu.VMEM((ROWS, HID), F32),
        pltpu.VMEM((48, D), BF16),
        pltpu.VMEM((ROWS, 1024), BF16),
        pltpu.VMEM((16, 64, 128), BF16),
        pltpu.VMEM((4, 4, 64, 128), BF16),
        pltpu.VMEM((16, 64, 128), BF16),
        pltpu.VMEM((16, 8, 128), F32),
        pltpu.VMEM((2, PH * TK), F32),
        pltpu.VMEM((2, PH * TK), F32),
        pltpu.VMEM((4, 2, PH * TK), F32),
        pltpu.VMEM((4, 2, PH * TK), F32),
        pltpu.VMEM((FEAT, PH * TK), F32),
        pltpu.VMEM((FEAT, PH * TK), F32),
        pltpu.VMEM((16, 32, 128), BF16),
        pltpu.VMEM((16, 32, 128), BF16),
        pltpu.VMEM((16, 32, 128), BF16),
        pltpu.VMEM((16, 32, 128), BF16),
        pltpu.VMEM((4, ROWS, 256), F32),
        pltpu.VMEM((4, ROWS, 256), F32),
        pltpu.VMEM((PAD, 256), BF16),
        pltpu.VMEM((4, PAD, 256), BF16),
        pltpu.VMEM((ROWS, 256), F32),
        pltpu.VMEM((4, ROWS, 256), F32),
        pltpu.VMEM((ROWS, 1024), F32),
        pltpu.VMEM((ROWS, 1024), F32),
        dma((11,)), dma((2 + NCH,)),
        dma((PH,)), dma((PH, 2)), dma((PH, 2)), dma((PH, 3, 2)), dma((PH, 2)), dma((PH,)),
        dma((1,)), dma((1,)),
        dma((2,)), dma((2,)), dma((2,)), dma((2,)), dma((2,)), dma((2,)),
        dma((NCH,)), dma((NCH,)),
        dma((4,)), dma((4,)), dma((4,)), dma((4,)), dma((4,)), dma((4,)),
    ]
    normed, adam, outer = pl.pallas_call(
        body,
        out_shape=(
            jax.ShapeDtypeStruct((48, D), BF16),
            jax.ShapeDtypeStruct((ROWS, HID), BF16),
            jax.ShapeDtypeStruct((ROWS, 1024), F32),
        ),
        in_specs=[hbm] * 9,
        out_specs=(hbm, hbm, hbm),
        scratch_shapes=scratch,
        compiler_params=pltpu.CompilerParams(
            collective_id=0, has_side_effects=True, vmem_limit_bytes=63 << 20
        ),
        cost_estimate=pl.CostEstimate(flops=2 * 10**9, bytes_accessed=4 * 10**6, transcendentals=0),
    )(
        hidden, down_w[0], m1[0], m2[0], gain, cot, delta[0],
        outer_params, outer_momentum,
    )
    return place(normed, adam[None], outer)


def solution(mesh):
    placed = (
        P(("group", "fsdp"), None),
        P("group", "fsdp", None),
        P("group", "fsdp", None),
        P("group", "fsdp", None),
        P(),
        P(("group", "fsdp"), None),
        P("group", "fsdp", None),
        P("fsdp", None),
        P("fsdp", None),
    )
    return jax.shard_map(
        per_device,
        mesh=mesh,
        in_specs=placed,
        out_specs=(P(("group", "fsdp"), None), P("group", "fsdp", None), P("fsdp", None)),
        check_vma=False,
    )
```
